32 devices in a mesh: req: 4 (over y, x), exp: 8 (over z, core).
Axes of the slice: x: 2, y: 2, z: 4, core: 2. Of those that a mesh axis runs over, the one named last changes fastest.
Arguments:
- hidden_in: bfloat16 [4096, 1536], P(('req', 'exp')), may hold values from -6 to 6
- attn_gain: bfloat16 [1536], replicated, may hold values from 0.099609375 to 1.8984375
- w_query: bfloat16 [1536, 1536], replicated, may hold values from -0.625 to 0.625
- w_key: bfloat16 [1536, 512], replicated, may hold values from -0.625 to 0.625
- w_value: bfloat16 [1536, 512], replicated, may hold values from -0.15625 to 0.15625
- w_out: bfloat16 [1536, 1536], replicated, may hold values from -0.15625 to 0.15625
- cache_kv: bfloat16 [4, 384, 1024], P('req', 'exp'), may hold values from -128 to 128
- cache_len: int32 [4], P('req'), may hold values from 12 to 384, as said below
- moe_gain: bfloat16 [1536], replicated, may hold values from 0.099609375 to 1.8984375
- expert_ids: int32 [4096, 8], P(('req', 'exp')), may hold values from 0 to 39, all different within a row; in each aligned block of 128 rows (0 to 127, 128 to 255, ...) at most 26 rows name the same one
- expert_weights: bfloat16 [4096, 8], P(('req', 'exp')), may hold values from 0.019897461 to 0.5
- w_gate_up: bfloat16 [8, 20, 1536, 256], P('exp', None, 'req'), may hold values from -0.15625 to 0.15625
- w_down: bfloat16 [8, 20, 128, 1536], P('exp', None, None, 'req'), may hold values from -0.25 to 0.25
Outputs:
- attended: bfloat16 [4096, 1536], P(('req', 'exp'))
- layer_out: bfloat16 [4096, 1536], P(('req', 'exp'))
The draws below stay inside these ranges and needn't reach their ends.
Inputs may be any that keep to these rules, and one draw needn't show every extreme that they name: `cache_len`: cached positions of each request; some request has exactly 384, some exactly 12. `expert_ids`: each row names 8 different experts. Among the rows of one device no expert is named more than 26 times; in some devices' rows one expert is named exactly 26 times.
All inputs are finite; a program needn't handle non-finite values.
Results may differ from the reference program's by a relative error of at most 0.009.
Values may be sent and summed in bfloat16 or wider, within the bound.
A program may use at most 256 MiB of HBM per device.

```python
import math
import jax
import jax.numpy as jnp
import numpy as np
from jax import lax

D = 1536
HEADS = 24
KV_HEADS = 8
HEAD_DIM = 64
EXPERTS = 40
FF = 512
TOPK = 8
PIECES = 4
SLICE = 128
GROUP_EXPERTS = 20
TOK_DEV = 128
MOST = 26
NEW = 1024
CACHE = 384
REQS = 4
TOKENS = 4096
N_EXP = 8


def draw_cache_kv(key, part):
    kv_width = KV_HEADS * HEAD_DIM
    key_main = jax.random.fold_in(key, 0)
    column_scale = jnp.concatenate([jnp.full((kv_width,), 4.0, jnp.float32), jnp.ones((kv_width,), jnp.float32)])
    draws = jnp.clip(jax.random.normal(key_main, (REQS, CACHE, 2 * kv_width), jnp.float32), -4.0, 4.0)
    values = draws * column_scale[None, None, :]
    return values.astype(jnp.bfloat16)


def draw_cache_len(key, part):
    key_len, key_order = jax.random.split(key)
    shortest = max(CACHE // 32, 2)
    lengths = jax.random.randint(key_len, (REQS,), shortest, CACHE + 1, jnp.int32)
    ranking = jax.random.permutation(key_order, REQS)
    return lengths.at[ranking[0]].set(CACHE).at[ranking[1]].set(shortest)


def steps_of(key, dims, shards, smallest, high):
    def one(dim, shards_of):
        steps = jax.random.uniform(jax.random.fold_in(jax.random.fold_in(key, 6), dim), (shards_of,), jnp.float32, smallest / len(shards), high / len(shards))
        return jnp.repeat(jnp.exp(steps), dims[dim] // shards_of).reshape((-1,) + (1,) * (len(dims) - dim - 1))

    level = one(*shards[0])
    for cut in shards[1:]:
        level = level * one(*cut)
    return level


def routed_block(rng, own, number, rows, count, top, limit, skew):
    sequence = jax.random.permutation(rng, count)
    packed, common = portions_of(count, rows * top, limit, skew, True), portions_of(count, rows * top, limit, skew, False)
    places = jnp.arange(count)

    def named(sizes, rotation):
        used = int((sizes > 0).sum())
        fixed = max(1, used // 4)
        moved = fixed + (places - fixed + rotation * (used - fixed)) % max(1, count - fixed)
        return jnp.zeros((count,), jnp.int32).at[sequence[jnp.where(places < fixed, places, moved)]].set(jnp.asarray(sizes, jnp.int32))

    sizes = jnp.where(number % 4 == 0, named(packed, number // 4), named(common, number - number // 4 - 1))
    mixed = jax.random.permutation(jax.random.fold_in(own, 3), count)
    giver, receiver = mixed[0:count // 2 * 2:2], mixed[1:count // 2 * 2:2]
    slack = jnp.minimum(sizes[giver] - 1, limit - sizes[receiver]) // 2
    slack = jnp.where((giver == sequence[0]) | (receiver == sequence[0]) | (sizes[receiver] == 0), 0, jnp.maximum(slack, 0))
    moved = jax.random.randint(jax.random.fold_in(own, 4), (count // 2,), 0, 1 << 20) % (slack + 1)
    sizes = sizes.at[giver].add(-moved).at[receiver].add(moved)
    members = jnp.searchsorted(jnp.cumsum(sizes), jnp.arange(rows * top), side="right").astype(jnp.int32)
    listing = members.reshape(top, rows).T
    listing = listing[jax.random.permutation(jax.random.fold_in(own, 1), rows)]
    rotation = jax.random.randint(jax.random.fold_in(own, 2), (rows, 1), 0, top)
    return jnp.take_along_axis(listing, (jnp.arange(top)[None, :] + rotation) % top, axis=1)


def portions_of(amount, total, bound, slope, full):
    portions = [(1 << 20) // math.isqrt(rank ** slope) + 1 for rank in range(1, amount + 1)]
    largest = bound if full else min(bound, max(-(-total // amount), total * portions[0] // sum(portions)))
    least = 1 if total - largest >= amount - 1 else 0
    holding, rest = [largest] + [least] * (amount - 1), total - largest - least * (amount - 1)
    while rest > 0:
        movable = [i for i in range(1, amount) if holding[i] < largest] or [i for i in range(1, amount) if holding[i] < bound]
        whole, budget = sum([portions[i] for i in movable]), rest
        for i in movable:
            extra = min(bound - holding[i], max(1, budget * portions[i] // whole), rest)
            holding[i] = holding[i] + extra
            rest = rest - extra
    return np.array(holding)


def gaussian(rng, shape, deviation, limit, shards=(), held_as=jnp.bfloat16):
    result = deviation * jax.random.normal(rng, shape, jnp.float32)
    if shards:
        result = result * steps_of(rng, shape, shards, -0.22, 0.18)
    return jnp.clip(result, -limit, limit).astype(held_as)


def setup_inputs(seed: int = 0) -> dict:
    key_of = jax.random.split(jax.random.key(seed), 14)
    hidden_in = gaussian(key_of[0], (TOKENS, D), 1.0, 6.0, ((0, 32),))
    attn_gain = jnp.clip(1.0 + 0.18 * jax.random.normal(key_of[1], (D,), jnp.float32), 0.099609375, 1.8984375).astype(jnp.bfloat16)
    w_query = gaussian(key_of[2], (D, HEADS * HEAD_DIM), (D // 16) ** -0.5, 0.625)
    w_key = gaussian(key_of[3], (D, KV_HEADS * HEAD_DIM), (D // 16) ** -0.5, 0.625)
    w_value = gaussian(key_of[4], (D, KV_HEADS * HEAD_DIM), D ** -0.5, 0.15625)
    w_out = gaussian(key_of[5], (HEADS * HEAD_DIM, D), (HEADS * HEAD_DIM) ** -0.5, 0.15625)
    cache_kv = draw_cache_kv(jax.random.fold_in(key_of[13], 71), 0)
    cache_len = draw_cache_len(jax.random.fold_in(key_of[13], 71), 0)
    moe_gain = jnp.clip(1.0 + 0.18 * jax.random.normal(key_of[8], (D,), jnp.float32), 0.099609375, 1.8984375).astype(jnp.bfloat16)
    expert_ids_keys = jax.random.split(jax.random.fold_in(key_of[9], 1), TOKENS // TOK_DEV)
    expert_ids_turns = jax.random.permutation(jax.random.fold_in(key_of[9], 3), TOKENS // TOK_DEV)
    expert_ids = jax.vmap(lambda own, number: routed_block(jax.random.fold_in(key_of[9], 2), own, number, TOK_DEV, EXPERTS, TOPK, MOST, 1))(expert_ids_keys, expert_ids_turns).reshape((TOKENS, TOPK))
    expert_weights = jnp.clip(jnp.exp(math.log(0.5) - 3.224016 * jax.random.uniform(key_of[10], (TOKENS, TOPK), jnp.float32) ** steps_of(key_of[10], (TOKENS, TOPK), ((0, 32),), -0.2, 0.2)), 0.019897461, 0.5).astype(jnp.bfloat16)
    w_gate_up = gaussian(key_of[11], (N_EXP, GROUP_EXPERTS, D, 2 * SLICE), D ** -0.5, 0.15625, ((0, 8), (2, 4)))
    w_down = gaussian(key_of[12], (N_EXP, GROUP_EXPERTS, SLICE, D), FF ** -0.5, 0.25, ((0, 8), (3, 4)))
    return {"hidden_in": hidden_in, "attn_gain": attn_gain, "w_query": w_query, "w_key": w_key, "w_value": w_value, "w_out": w_out, "cache_kv": cache_kv, "cache_len": cache_len, "moe_gain": moe_gain, "expert_ids": expert_ids, "expert_weights": expert_weights, "w_gate_up": w_gate_up, "w_down": w_down}


rope_base = 10000.0
attn_scale = 0.015625
residual_scale = 1.0
norm_eps = 1e-06
neg_fill = -1e+30

def rms_scale(values, gain):
    widened = values.astype(jnp.float32)
    mean_sq = lax.optimization_barrier(jnp.mean(widened * widened, axis=-1, keepdims=True))
    return (widened * lax.rsqrt(mean_sq + norm_eps) * gain.astype(jnp.float32)).astype(jnp.bfloat16)

def rotate(projected, positions, head_count, head_dim):
    row_count = projected.shape[0]
    shaped = projected.reshape(row_count, head_count, head_dim)
    half_dim = head_dim // 2
    inverse_freq = rope_base ** (-(jnp.arange(half_dim, dtype=jnp.float32) * 2.0 / head_dim))
    angles = positions.astype(jnp.float32)[:, None] * inverse_freq[None, :]
    cosine = jnp.cos(angles)[:, None, :]
    sinus = jnp.sin(angles)[:, None, :]
    lower_half = shaped[..., :half_dim]
    upper_half = shaped[..., half_dim:]
    turned = jnp.concatenate([lower_half * cosine - upper_half * sinus, upper_half * cosine + lower_half * sinus], axis=-1)
    return turned.reshape(row_count, head_count * head_dim).astype(jnp.bfloat16)

def attend_request(query, key_rows, value_rows, length):
    new_total = query.shape[0]
    group_size = HEADS // KV_HEADS
    key_count = key_rows.shape[0]
    key_heads = key_rows.astype(jnp.float32).reshape(key_count, KV_HEADS, HEAD_DIM)
    value_heads = value_rows.astype(jnp.float32).reshape(key_count, KV_HEADS, HEAD_DIM)
    key_index = jnp.arange(key_count, dtype=jnp.int32)
    block_rows = min(512, new_total)

    def one_block(first_row):
        query_block = lax.dynamic_slice_in_dim(query, first_row, block_rows, 0).astype(jnp.float32)
        query_block = query_block.reshape(block_rows, KV_HEADS, group_size, HEAD_DIM)
        scores = jnp.einsum('tkgd,rkd->tkgr', query_block, key_heads) * attn_scale
        query_index = first_row + jnp.arange(block_rows, dtype=jnp.int32)
        visible = jnp.where(key_index[None, :] < CACHE, (key_index < length)[None, :], (key_index - CACHE)[None, :] <= query_index[:, None])
        scores = jnp.where(visible[:, None, None, :], scores, neg_fill)
        top_score = lax.optimization_barrier(jnp.max(scores, axis=-1, keepdims=True))
        weights = jnp.where(visible[:, None, None, :], jnp.exp(scores - top_score), 0.0)
        total_sum = lax.optimization_barrier(jnp.sum(weights, axis=-1))
        rounded = lax.optimization_barrier(weights.astype(jnp.bfloat16)).astype(jnp.float32)
        context = jnp.einsum('tkgr,rkd->tkgd', rounded, value_heads) / total_sum[..., None]
        return context.reshape(block_rows, HEADS * HEAD_DIM).astype(jnp.bfloat16)
    starts = jnp.arange(new_total // block_rows, dtype=jnp.int32) * block_rows
    return lax.map(one_block, starts).reshape(new_total, HEADS * HEAD_DIM)

def reference(hidden_in, attn_gain, w_query, w_key, w_value, w_out, cache_kv, cache_len, moe_gain, expert_ids, expert_weights, w_gate_up, w_down):
    kv_width = KV_HEADS * HEAD_DIM
    normed = rms_scale(hidden_in, attn_gain)
    token_index = jnp.arange(NEW, dtype=jnp.int32)
    contexts = []
    for request in range(REQS):
        request_rows = normed[request * NEW:(request + 1) * NEW]
        positions = cache_len[request] + token_index
        query = rotate(jnp.dot(request_rows, w_query, preferred_element_type=jnp.float32), positions, HEADS, HEAD_DIM)
        keys_new = rotate(jnp.dot(request_rows, w_key, preferred_element_type=jnp.float32), positions, KV_HEADS, HEAD_DIM)
        values_new = jnp.dot(request_rows, w_value, preferred_element_type=jnp.float32).astype(jnp.bfloat16)
        key_rows = jnp.concatenate([cache_kv[request, :, :kv_width], keys_new], axis=0)
        value_rows = jnp.concatenate([cache_kv[request, :, kv_width:], values_new], axis=0)
        contexts.append(attend_request(query, key_rows, value_rows, cache_len[request]))
    context = jnp.concatenate(contexts, axis=0)
    projected = jnp.dot(context, w_out, preferred_element_type=jnp.float32)
    attended = (hidden_in.astype(jnp.float32) + residual_scale * projected).astype(jnp.bfloat16)
    moe_in = rms_scale(attended, moe_gain)
    blocks = N_EXP // PIECES
    gate_up = w_gate_up.reshape(blocks, PIECES, GROUP_EXPERTS, D, 2 * SLICE).transpose(0, 2, 1, 3, 4).reshape(EXPERTS, PIECES, D, 2 * SLICE)
    down_rows = w_down.reshape(blocks, PIECES, GROUP_EXPERTS, SLICE, D).transpose(0, 2, 1, 3, 4).reshape(EXPERTS, PIECES, SLICE, D)
    flat_ids = expert_ids.reshape(-1)
    flat_weights = expert_weights.reshape(-1).astype(jnp.float32)
    pair_count = flat_ids.shape[0]
    token_of = jnp.arange(pair_count, dtype=jnp.int32) // TOPK
    ranking = jnp.argsort(flat_ids, stable=True).astype(jnp.int32)
    expert_loads = lax.optimization_barrier(jnp.sum((flat_ids[:, None] == jnp.arange(EXPERTS, dtype=jnp.int32)[None, :]).astype(jnp.int32), axis=0))
    offsets = jnp.cumsum(expert_loads) - expert_loads
    capacity = TOKENS // TOK_DEV * MOST
    slot_rank = jnp.arange(capacity, dtype=jnp.int32)
    occupied = slot_rank[None, :] < expert_loads[:, None]
    chosen = ranking[jnp.minimum(offsets[:, None] + slot_rank[None, :], pair_count - 1)]
    tokens_sel = token_of[chosen]
    weight_sel = jnp.where(occupied, flat_weights[chosen], 0.0)

    def expert_step(running, inputs):
        gate_e, down_e, tokens_e, weight_e = inputs
        rows_e = moe_in[tokens_e].astype(jnp.float32)
        gated = jnp.einsum('cd,qdf->qcf', rows_e, gate_e.astype(jnp.float32))
        activ = (jax.nn.silu(gated[..., :SLICE]) * gated[..., SLICE:]).astype(jnp.bfloat16)
        activ = lax.optimization_barrier(activ).astype(jnp.float32)
        partial_value = jnp.einsum('qcf,qfd->qcd', activ, down_e.astype(jnp.float32)).astype(jnp.bfloat16)
        partial_value = lax.optimization_barrier(partial_value).astype(jnp.float32)
        weighted = weight_e[:, None] * lax.optimization_barrier(jnp.sum(partial_value, axis=0))
        return (running.at[tokens_e].add(weighted), None)
    mixture, _ = lax.scan(expert_step, jnp.zeros((TOKENS, D), jnp.float32), (gate_up, down_rows, tokens_sel, weight_sel))
    layer_out = (attended.astype(jnp.float32) + residual_scale * mixture).astype(jnp.bfloat16)
    return (attended, layer_out)
```

```python
import jax
import jax.numpy as jnp
from jax import lax
from jax.experimental import pallas as pl
from jax.experimental.pallas import tpu as pltpu
from jax.sharding import PartitionSpec as P

HEAD_DIM = 64
PIECES = 4
ROUTE_LANES = 128


rope_base = 10000.0
attn_scale = 0.015625
residual_scale = 1.0
norm_eps = 1e-06
neg_fill = -1e30
key_block = 512


def rms_scale(values, gain):
    widened = values.astype(jnp.float32)
    mean_sq = jnp.mean(widened * widened, axis=-1, keepdims=True)
    return (widened * lax.rsqrt(mean_sq + norm_eps) * gain.astype(jnp.float32)).astype(jnp.bfloat16)


def rotate(projected, positions, head_count, head_dim):
    row_count = projected.shape[0]
    shaped = projected.reshape(row_count, head_count, head_dim)
    half_dim = head_dim // 2
    inverse_freq = rope_base ** (-(jnp.arange(half_dim, dtype=jnp.float32) * 2.0 / head_dim))
    angles = positions.astype(jnp.float32)[:, None] * inverse_freq[None, :]
    cosine = jnp.cos(angles)[:, None, :]
    sinus = jnp.sin(angles)[:, None, :]
    lower_half = shaped[..., :half_dim]
    upper_half = shaped[..., half_dim:]
    turned = jnp.concatenate(
        [lower_half * cosine - upper_half * sinus, upper_half * cosine + lower_half * sinus],
        axis=-1,
    )
    return turned.reshape(row_count, head_count * head_dim).astype(jnp.bfloat16)


def attend_block(running, queries, block_rows, visible, kv_width):
    run_max, run_sum, run_acc = running
    kv_heads = run_max.shape[0]
    head_dim = run_acc.shape[-1]
    block_size = block_rows.shape[0]
    key_heads = block_rows[:, :kv_width].reshape(block_size, kv_heads, head_dim)
    value_heads = block_rows[:, kv_width:].reshape(block_size, kv_heads, head_dim)
    scores = (
        jnp.einsum("tkgd,rkd->kgtr", queries, key_heads, preferred_element_type=jnp.float32)
        * attn_scale
    )
    scores = jnp.where(visible[None, None], scores, neg_fill)
    new_max = jnp.maximum(run_max, jnp.max(scores, axis=-1))
    weights = jnp.where(visible[None, None], jnp.exp(scores - new_max[..., None]), 0.0)
    factor = jnp.exp(run_max - new_max)
    new_sum = run_sum * factor + jnp.sum(weights, axis=-1)
    new_acc = run_acc * factor[..., None] + jnp.einsum(
        "kgtr,rkd->kgtd",
        weights.astype(jnp.bfloat16),
        value_heads,
        preferred_element_type=jnp.float32,
    )
    return (new_max, new_sum, new_acc)


def shards(
    hidden_in,
    attn_gain,
    w_query,
    w_key,
    w_value,
    w_out,
    cache_kv,
    cache_len,
    moe_gain,
    expert_ids,
    expert_weights,
    w_gate_up,
    w_down,
):
    rows_here = hidden_in.shape[0]
    width = hidden_in.shape[1]
    kv_width = w_key.shape[1]
    kv_heads = kv_width // HEAD_DIM
    head_count = w_query.shape[1] // HEAD_DIM
    group_size = head_count // kv_heads
    position_exp = lax.axis_index("exp")
    length = cache_len[0]
    cache_rows = cache_kv[0]
    cache_count = cache_rows.shape[0]
    gate_up_full, down_full = (
        lax.all_gather(w_gate_up[0], "req", axis=0),
        lax.all_gather(w_down[0], "req", axis=0),
    )
    normed = rms_scale(hidden_in, attn_gain)
    query_pos = position_exp * rows_here + jnp.arange(rows_here, dtype=jnp.int32)
    positions = length + query_pos
    query = rotate(
        jnp.dot(normed, w_query, preferred_element_type=jnp.float32),
        positions,
        head_count,
        HEAD_DIM,
    )
    keys_new = rotate(
        jnp.dot(normed, w_key, preferred_element_type=jnp.float32), positions, kv_heads, HEAD_DIM
    )
    values_new = jnp.dot(normed, w_value, preferred_element_type=jnp.float32).astype(jnp.bfloat16)
    new_kv = jnp.concatenate([keys_new, values_new], axis=1)
    queries = query.reshape(rows_here, kv_heads, group_size, HEAD_DIM)
    initial = (
        jnp.full((kv_heads, group_size, rows_here), neg_fill, jnp.float32),
        jnp.zeros((kv_heads, group_size, rows_here), jnp.float32),
        jnp.zeros((kv_heads, group_size, rows_here, HEAD_DIM), jnp.float32),
    )
    shard_rows = cache_count + rows_here
    joined = jnp.concatenate([cache_rows, new_kv], axis=0)
    running = initial
    piece = lax.all_gather(joined, "exp", axis=0, tiled=True)
    first_row = jnp.int32(0)
    key_count = piece.shape[0]
    for offset in range(0, key_count, key_block):
        block_size = min(key_block, key_count - offset)
        key_index = first_row + offset + jnp.arange(block_size, dtype=jnp.int32)
        owner = key_index // shard_rows
        within = key_index - owner * shard_rows
        cached = within < cache_count
        cache_pos = owner * cache_count + within
        new_pos = owner * rows_here + within - cache_count
        running = attend_block(
            running,
            queries,
            piece[offset : offset + block_size],
            jnp.where(
                cached[None, :],
                (cache_pos < length)[None, :],
                new_pos[None, :] <= query_pos[:, None],
            ),
            kv_width,
        )
    run_max, run_sum, run_acc = running
    context = (
        (run_acc / run_sum[..., None])
        .transpose(2, 0, 1, 3)
        .reshape(rows_here, head_count * HEAD_DIM)
        .astype(jnp.bfloat16)
    )
    projected = jnp.dot(context, w_out, preferred_element_type=jnp.float32)
    attended = (hidden_in.astype(jnp.float32) + residual_scale * projected).astype(jnp.bfloat16)
    moe_in = rms_scale(attended, moe_gain)
    block_experts = w_gate_up.shape[1]
    group = lax.axis_index("exp") // PIECES
    named = expert_ids[:, :, None] == jnp.arange(ROUTE_LANES, dtype=jnp.int32)[None, None, :]
    routing = jnp.sum(
        jnp.where(named, expert_weights.astype(jnp.float32)[:, :, None], 0.0), axis=1
    ).astype(jnp.bfloat16)
    gathered = lax.all_gather(
        jnp.concatenate([moe_in, routing], axis=1), "exp", axis=0, tiled=True
    )
    partial = expert_sums(
        group * block_experts, gathered, gate_up_full, down_full, width, block_experts
    )
    mixture = lax.psum_scatter(partial, "exp", scatter_dimension=0, tiled=True)
    layer_out = (
        attended.astype(jnp.float32) + residual_scale * mixture.astype(jnp.float32)
    ).astype(jnp.bfloat16)
    return (attended, layer_out)


def expert_kernel(first_ref, rows_ref, route_ref, gate_up_ref, down_ref, out_ref, total):
    step = pl.program_id(1)
    per_step = gate_up_ref.shape[1]
    slice_width = down_ref.shape[2]
    rows = rows_ref[...]
    route = route_ref[...]
    lane = lax.broadcasted_iota(jnp.int32, (ROUTE_LANES, slice_width), 0)
    acts = []
    for k in range(per_step):
        weights = gate_up_ref[:, k].reshape(rows.shape[1], 2 * slice_width)
        hidden = jnp.dot(rows, weights, preferred_element_type=jnp.float32)
        gate, up = hidden[:, :slice_width], hidden[:, slice_width:]
        pick = (lane == first_ref[0] + step * per_step + k).astype(jnp.bfloat16)
        weight = jnp.dot(route, pick, preferred_element_type=jnp.float32)
        acts.append((gate / (1.0 + jnp.exp(-gate)) * up * weight).astype(jnp.bfloat16))
    act = jnp.concatenate(acts, axis=1)
    parts = down_ref.shape[0]
    columns = down_ref.shape[3]
    for part in range(parts):
        down = down_ref[part].reshape(per_step * slice_width, columns)
        made = jnp.dot(act, down, preferred_element_type=jnp.float32)
        where = slice(part * columns, (part + 1) * columns)

        @pl.when(step == 0)
        def _():
            total[:, where] = made

        @pl.when(step > 0)
        def _():
            total[:, where] += made

    @pl.when(step == pl.num_programs(1) - 1)
    def _():
        out_ref[...] = total[...].astype(out_ref.dtype)


def expert_sums(first, gathered, gate_up, down, width, block_experts):
    count = gathered.shape[0]
    tile = min(1024, count)
    per_step = 2 if block_experts % 2 == 0 else 1
    parts, _, depth, wide = gate_up.shape
    _, _, slice_width, columns = down.shape
    return pl.pallas_call(
        expert_kernel,
        grid_spec=pltpu.PrefetchScalarGridSpec(
            num_scalar_prefetch=1,
            grid=(count // tile, block_experts // per_step),
            in_specs=[
                pl.BlockSpec((tile, width), lambda i, s, first: (i, 0)),
                pl.BlockSpec((tile, ROUTE_LANES), lambda i, s, first: (i, width // ROUTE_LANES)),
                pl.BlockSpec((parts, per_step, depth, wide), lambda i, s, first: (0, s, 0, 0)),
                pl.BlockSpec(
                    (parts, per_step, slice_width, columns), lambda i, s, first: (0, s, 0, 0)
                ),
            ],
            out_specs=pl.BlockSpec((tile, width), lambda i, s, first: (i, 0)),
            scratch_shapes=[pltpu.VMEM((tile, width), jnp.float32)],
        ),
        out_shape=jax.ShapeDtypeStruct((count, width), jnp.bfloat16),
        compiler_params=pltpu.CompilerParams(vmem_limit_bytes=50 * 1024 * 1024),
        cost_estimate=pl.CostEstimate(
            flops=6 * count * width * block_experts * slice_width,
            bytes_accessed=6 * block_experts * width * slice_width + 4 * count * width,
            transcendentals=count * block_experts * slice_width,
        ),
    )(jnp.full((1,), first, jnp.int32), gathered, gathered, gate_up, down)


def solution(mesh):
    in_specs = (
        P(("req", "exp"), None),
        P(),
        P(),
        P(),
        P(),
        P(),
        P("req", "exp", None),
        P("req"),
        P(),
        P(("req", "exp"), None),
        P(("req", "exp"), None),
        P("exp", None, "req", None),
        P("exp", None, None, "req"),
    )
    out_specs = (P(("req", "exp"), None), P(("req", "exp"), None))
    return jax.shard_map(shards, mesh=mesh, in_specs=in_specs, out_specs=out_specs, check_vma=False)
```

```python
import functools

import jax
import jax.numpy as jnp
from jax import lax
from jax.experimental import pallas as pl
from jax.experimental.pallas import tpu as pltpu
from jax.sharding import PartitionSpec as P

HEAD_DIM = 64
PIECES = 4
ROUTE_LANES = 128
REQ_PARTS = 4


rope_base = 10000.0
attn_scale = 0.015625
residual_scale = 1.0
norm_eps = 1e-06
neg_fill = -1e30
key_block = 512


def rms_scale(values, gain):
    widened = values.astype(jnp.float32)
    mean_sq = jnp.mean(widened * widened, axis=-1, keepdims=True)
    return (widened * lax.rsqrt(mean_sq + norm_eps) * gain.astype(jnp.float32)).astype(jnp.bfloat16)


def rotate(projected, positions, head_count, head_dim):
    row_count = projected.shape[0]
    shaped = projected.reshape(row_count, head_count, head_dim)
    half_dim = head_dim // 2
    inverse_freq = rope_base ** (-(jnp.arange(half_dim, dtype=jnp.float32) * 2.0 / head_dim))
    angles = positions.astype(jnp.float32)[:, None] * inverse_freq[None, :]
    cosine = jnp.cos(angles)[:, None, :]
    sinus = jnp.sin(angles)[:, None, :]
    lower_half = shaped[..., :half_dim]
    upper_half = shaped[..., half_dim:]
    turned = jnp.concatenate(
        [lower_half * cosine - upper_half * sinus, upper_half * cosine + lower_half * sinus],
        axis=-1,
    )
    return turned.reshape(row_count, head_count * head_dim).astype(jnp.bfloat16)


def attend_block(running, queries, block_rows, visible, kv_width):
    run_max, run_sum, run_acc = running
    kv_heads = run_max.shape[0]
    head_dim = run_acc.shape[-1]
    block_size = block_rows.shape[0]
    key_heads = block_rows[:, :kv_width].reshape(block_size, kv_heads, head_dim)
    value_heads = block_rows[:, kv_width:].reshape(block_size, kv_heads, head_dim)
    scores = (
        jnp.einsum("tkgd,rkd->kgtr", queries, key_heads, preferred_element_type=jnp.float32)
        * attn_scale
    )
    scores = jnp.where(visible[None, None], scores, neg_fill)
    new_max = jnp.maximum(run_max, jnp.max(scores, axis=-1))
    weights = jnp.where(visible[None, None], jnp.exp(scores - new_max[..., None]), 0.0)
    factor = jnp.exp(run_max - new_max)
    new_sum = run_sum * factor + jnp.sum(weights, axis=-1)
    new_acc = run_acc * factor[..., None] + jnp.einsum(
        "kgtr,rkd->kgtd",
        weights.astype(jnp.bfloat16),
        value_heads,
        preferred_element_type=jnp.float32,
    )
    return (new_max, new_sum, new_acc)


def shards(
    hidden_in,
    attn_gain,
    w_query,
    w_key,
    w_value,
    w_out,
    cache_kv,
    cache_len,
    moe_gain,
    expert_ids,
    expert_weights,
    w_gate_up,
    w_down,
):
    rows_here = hidden_in.shape[0]
    width = hidden_in.shape[1]
    kv_width = w_key.shape[1]
    kv_heads = kv_width // HEAD_DIM
    head_count = w_query.shape[1] // HEAD_DIM
    group_size = head_count // kv_heads
    position_exp = lax.axis_index("exp")
    length = cache_len[0]
    cache_rows = cache_kv[0]
    cache_count = cache_rows.shape[0]
    half = (w_gate_up.shape[1] + 1) // 2
    low, high = w_gate_up[0, :half], w_gate_up[0, half:]
    low_1, low_2 = swap(low, 1), swap(low, 2)
    normed = rms_scale(hidden_in, attn_gain)
    query_pos = position_exp * rows_here + jnp.arange(rows_here, dtype=jnp.int32)
    positions = length + query_pos
    query = rotate(
        jnp.dot(normed, w_query, preferred_element_type=jnp.float32),
        positions,
        head_count,
        HEAD_DIM,
    )
    keys_new = rotate(
        jnp.dot(normed, w_key, preferred_element_type=jnp.float32), positions, kv_heads, HEAD_DIM
    )
    values_new = jnp.dot(normed, w_value, preferred_element_type=jnp.float32).astype(jnp.bfloat16)
    new_kv = jnp.concatenate([keys_new, values_new], axis=1)
    queries = query.reshape(rows_here, kv_heads, group_size, HEAD_DIM)
    initial = (
        jnp.full((kv_heads, group_size, rows_here), neg_fill, jnp.float32),
        jnp.zeros((kv_heads, group_size, rows_here), jnp.float32),
        jnp.zeros((kv_heads, group_size, rows_here, HEAD_DIM), jnp.float32),
    )
    shard_rows = cache_count + rows_here
    joined = jnp.concatenate([cache_rows, new_kv], axis=0)
    running = initial
    piece = lax.all_gather(joined, "exp", axis=0, tiled=True)
    piece, low_1, low_2 = lax.optimization_barrier((piece, low_1, low_2))
    high_1, high_2 = swap(high, 1), swap(high, 2)
    first_row = jnp.int32(0)
    key_count = piece.shape[0]
    for offset in range(0, key_count, key_block):
        block_size = min(key_block, key_count - offset)
        key_index = first_row + offset + jnp.arange(block_size, dtype=jnp.int32)
        owner = key_index // shard_rows
        within = key_index - owner * shard_rows
        cached = within < cache_count
        cache_pos = owner * cache_count + within
        new_pos = owner * rows_here + within - cache_count
        running = attend_block(
            running,
            queries,
            piece[offset : offset + block_size],
            jnp.where(
                cached[None, :],
                (cache_pos < length)[None, :],
                new_pos[None, :] <= query_pos[:, None],
            ),
            kv_width,
        )
    run_max, run_sum, run_acc = running
    context = (
        (run_acc / run_sum[..., None])
        .transpose(2, 0, 1, 3)
        .reshape(rows_here, head_count * HEAD_DIM)
        .astype(jnp.bfloat16)
    )
    projected = jnp.dot(context, w_out, preferred_element_type=jnp.float32)
    attended = (hidden_in.astype(jnp.float32) + residual_scale * projected).astype(jnp.bfloat16)
    moe_in = rms_scale(attended, moe_gain)
    moe_in, high_1, high_2 = lax.optimization_barrier((moe_in, high_1, high_2))
    low_3 = swap(low_2, 1)
    high_3 = swap(high_1, 2)
    block_experts = w_gate_up.shape[1]
    group = lax.axis_index("exp") // PIECES
    named = expert_ids[:, :, None] == jnp.arange(ROUTE_LANES, dtype=jnp.int32)[None, None, :]
    routing = jnp.sum(
        jnp.where(named, expert_weights.astype(jnp.float32)[:, :, None], 0.0), axis=1
    ).astype(jnp.bfloat16)
    part = width // REQ_PARTS
    own = lax.axis_index("req")
    sent = [
        lax.dynamic_slice_in_dim(moe_in, (own ^ flip) * part, part, 1)
        for flip in range(REQ_PARTS)
    ]
    gathered = lax.all_gather(
        jnp.concatenate(sent + [routing], axis=1), "exp", axis=0, tiled=True
    )
    first = group * block_experts
    act_low = expert_acts(first, gathered, (low, low_1, low_2, low_3), width)
    act_high = expert_acts(first + half, gathered, (high, high_1, high_2, high_3), width)
    down, low_3, high_3 = lax.optimization_barrier((w_down[0], low_3, high_3))
    down_1, down_2 = swap(down, 1), swap(down, 2)
    down_3_low = swap(down_2[:half], 1)
    down_3_high = swap(down_1[half:], 2)
    act_high, down_3_low, down_3_high = lax.optimization_barrier(
        (act_high, down_3_low, down_3_high)
    )
    made = [
        jnp.dot(act_low, flat(rows[:half]), preferred_element_type=jnp.float32)
        + jnp.dot(act_high, flat(rows[half:]), preferred_element_type=jnp.float32)
        for rows in (down, down_1, down_2)
    ]
    made_3 = jnp.dot(act_low, flat(down_3_low), preferred_element_type=jnp.float32) + jnp.dot(
        act_high, flat(down_3_high), preferred_element_type=jnp.float32
    )
    mixed = jnp.concatenate(
        [
            lax.psum_scatter(
                jnp.concatenate(made, axis=1).astype(jnp.bfloat16),
                "exp",
                scatter_dimension=0,
                tiled=True,
            ),
            lax.psum_scatter(
                made_3.astype(jnp.bfloat16), "exp", scatter_dimension=0, tiled=True
            ),
        ],
        axis=1,
    )
    mixture = jnp.concatenate(
        [
            lax.dynamic_slice_in_dim(mixed, (own ^ flip) * part, part, 1)
            for flip in range(REQ_PARTS)
        ],
        axis=1,
    )
    layer_out = (
        attended.astype(jnp.float32) + residual_scale * mixture.astype(jnp.float32)
    ).astype(jnp.bfloat16)
    return (attended, layer_out)


def swap(values, flip):
    return lax.ppermute(values, "req", [(r, r ^ flip) for r in range(REQ_PARTS)])


def flat(rows):
    return rows.reshape(rows.shape[0] * rows.shape[1], rows.shape[2])


def act_kernel(per_step, first_ref, rows_ref, route_ref, *refs):
    step = pl.program_id(1)
    gate_up_refs, out_ref = refs[:-1], refs[-1]
    slice_width = gate_up_refs[0].shape[2] // 2
    rows = rows_ref[...]
    route = route_ref[...]
    lane = lax.broadcasted_iota(jnp.int32, (ROUTE_LANES, slice_width), 0)
    for k in range(per_step):
        weights = jnp.concatenate([ref[k] for ref in gate_up_refs], axis=0)
        hidden = jnp.dot(rows, weights, preferred_element_type=jnp.float32)
        gate, up = hidden[:, :slice_width], hidden[:, slice_width:]
        pick = (lane == first_ref[0] + step * per_step + k).astype(jnp.bfloat16)
        weight = jnp.dot(route, pick, preferred_element_type=jnp.float32)
        where = slice(k * slice_width, (k + 1) * slice_width)
        out_ref[:, where] = (gate / (1.0 + jnp.exp(-gate)) * up * weight).astype(out_ref.dtype)


def expert_acts(first, gathered, weights, width):
    count = gathered.shape[0]
    tile = min(1024, count)
    experts, depth, wide = weights[0].shape
    slice_width = wide // 2
    per_step = 2 if experts % 2 == 0 else 1
    in_specs = [
        pl.BlockSpec((tile, width), lambda i, s, first: (i, 0)),
        pl.BlockSpec((tile, ROUTE_LANES), lambda i, s, first: (i, width // ROUTE_LANES)),
    ]
    for _ in weights:
        in_specs.append(pl.BlockSpec((per_step, depth, wide), lambda i, s, first: (s, 0, 0)))
    return pl.pallas_call(
        functools.partial(act_kernel, per_step),
        grid_spec=pltpu.PrefetchScalarGridSpec(
            num_scalar_prefetch=1,
            grid=(count // tile, experts // per_step),
            in_specs=in_specs,
            out_specs=pl.BlockSpec((tile, per_step * slice_width), lambda i, s, first: (i, s)),
        ),
        out_shape=jax.ShapeDtypeStruct((count, experts * slice_width), jnp.bfloat16),
        compiler_params=pltpu.CompilerParams(vmem_limit_bytes=40 * 1024 * 1024),
        cost_estimate=pl.CostEstimate(
            flops=2 * count * width * experts * wide,
            bytes_accessed=2 * (experts * width * wide + count * (width + experts * slice_width)),
            transcendentals=count * experts * slice_width,
        ),
    )(jnp.full((1,), first, jnp.int32), gathered, gathered, *weights)


def solution(mesh):
    in_specs = (
        P(("req", "exp"), None),
        P(),
        P(),
        P(),
        P(),
        P(),
        P("req", "exp", None),
        P("req"),
        P(),
        P(("req", "exp"), None),
        P(("req", "exp"), None),
        P("exp", None, "req", None),
        P("exp", None, None, "req"),
    )
    out_specs = (P(("req", "exp"), None), P(("req", "exp"), None))
    return jax.shard_map(shards, mesh=mesh, in_specs=in_specs, out_specs=out_specs, check_vma=False)
```

```python
import functools

import jax
import jax.numpy as jnp
from jax import lax
from jax.experimental import pallas as pl
from jax.experimental.pallas import tpu as pltpu
from jax.sharding import PartitionSpec as P

HEAD_DIM = 64
PIECES = 4
ROUTE_LANES = 128
REQ_PARTS = 4


rope_base = 10000.0
attn_scale = 0.015625
residual_scale = 1.0
norm_eps = 1e-06
neg_fill = -1e30
key_block = 512


def rms_scale(values, gain):
    widened = values.astype(jnp.float32)
    mean_sq = jnp.mean(widened * widened, axis=-1, keepdims=True)
    return (widened * lax.rsqrt(mean_sq + norm_eps) * gain.astype(jnp.float32)).astype(jnp.bfloat16)


def rotate(projected, positions, head_count, head_dim):
    row_count = projected.shape[0]
    shaped = projected.reshape(row_count, head_count, head_dim)
    half_dim = head_dim // 2
    inverse_freq = rope_base ** (-(jnp.arange(half_dim, dtype=jnp.float32) * 2.0 / head_dim))
    angles = positions.astype(jnp.float32)[:, None] * inverse_freq[None, :]
    cosine = jnp.cos(angles)[:, None, :]
    sinus = jnp.sin(angles)[:, None, :]
    lower_half = shaped[..., :half_dim]
    upper_half = shaped[..., half_dim:]
    turned = jnp.concatenate(
        [lower_half * cosine - upper_half * sinus, upper_half * cosine + lower_half * sinus],
        axis=-1,
    )
    return turned.reshape(row_count, head_count * head_dim).astype(jnp.bfloat16)


def attend_block(running, queries, block_rows, visible, kv_width):
    run_max, run_sum, run_acc = running
    kv_heads = run_max.shape[0]
    head_dim = run_acc.shape[-1]
    block_size = block_rows.shape[0]
    key_heads = block_rows[:, :kv_width].reshape(block_size, kv_heads, head_dim)
    value_heads = block_rows[:, kv_width:].reshape(block_size, kv_heads, head_dim)
    scores = (
        jnp.einsum("tkgd,rkd->kgtr", queries, key_heads, preferred_element_type=jnp.float32)
        * attn_scale
    )
    scores = jnp.where(visible[None, None], scores, neg_fill)
    new_max = jnp.maximum(run_max, jnp.max(scores, axis=-1))
    weights = jnp.where(visible[None, None], jnp.exp(scores - new_max[..., None]), 0.0)
    factor = jnp.exp(run_max - new_max)
    new_sum = run_sum * factor + jnp.sum(weights, axis=-1)
    new_acc = run_acc * factor[..., None] + jnp.einsum(
        "kgtr,rkd->kgtd",
        weights.astype(jnp.bfloat16),
        value_heads,
        preferred_element_type=jnp.float32,
    )
    return (new_max, new_sum, new_acc)


def shards(
    hidden_in,
    attn_gain,
    w_query,
    w_key,
    w_value,
    w_out,
    cache_kv,
    cache_len,
    moe_gain,
    expert_ids,
    expert_weights,
    w_gate_up,
    w_down,
):
    rows_here = hidden_in.shape[0]
    width = hidden_in.shape[1]
    kv_width = w_key.shape[1]
    kv_heads = kv_width // HEAD_DIM
    head_count = w_query.shape[1] // HEAD_DIM
    group_size = head_count // kv_heads
    position_exp = lax.axis_index("exp")
    length = cache_len[0]
    cache_rows = cache_kv[0]
    cache_count = cache_rows.shape[0]
    half = (w_gate_up.shape[1] + 1) // 2
    low, high = w_gate_up[0, :half], w_gate_up[0, half:]
    low_1, low_2 = swap(low, 1), swap(low, 2)
    normed = rms_scale(hidden_in, attn_gain)
    query_pos = position_exp * rows_here + jnp.arange(rows_here, dtype=jnp.int32)
    positions = length + query_pos
    query = rotate(
        jnp.dot(normed, w_query, preferred_element_type=jnp.float32),
        positions,
        head_count,
        HEAD_DIM,
    )
    keys_new = rotate(
        jnp.dot(normed, w_key, preferred_element_type=jnp.float32), positions, kv_heads, HEAD_DIM
    )
    values_new = jnp.dot(normed, w_value, preferred_element_type=jnp.float32).astype(jnp.bfloat16)
    new_kv = jnp.concatenate([keys_new, values_new], axis=1)
    queries = query.reshape(rows_here, kv_heads, group_size, HEAD_DIM)
    initial = (
        jnp.full((kv_heads, group_size, rows_here), neg_fill, jnp.float32),
        jnp.zeros((kv_heads, group_size, rows_here), jnp.float32),
        jnp.zeros((kv_heads, group_size, rows_here, HEAD_DIM), jnp.float32),
    )
    shard_rows = cache_count + rows_here
    joined = jnp.concatenate([cache_rows, new_kv], axis=0)
    running = initial
    piece = lax.all_gather(joined, "exp", axis=0, tiled=True)
    piece, low_1, low_2 = lax.optimization_barrier((piece, low_1, low_2))
    high_1, high_2 = swap(high, 1), swap(high, 2)
    first_row = jnp.int32(0)
    key_count = piece.shape[0]
    for offset in range(0, key_count, key_block):
        block_size = min(key_block, key_count - offset)
        key_index = first_row + offset + jnp.arange(block_size, dtype=jnp.int32)
        owner = key_index // shard_rows
        within = key_index - owner * shard_rows
        cached = within < cache_count
        cache_pos = owner * cache_count + within
        new_pos = owner * rows_here + within - cache_count
        running = attend_block(
            running,
            queries,
            piece[offset : offset + block_size],
            jnp.where(
                cached[None, :],
                (cache_pos < length)[None, :],
                new_pos[None, :] <= query_pos[:, None],
            ),
            kv_width,
        )
    run_max, run_sum, run_acc = running
    context = (
        (run_acc / run_sum[..., None])
        .transpose(2, 0, 1, 3)
        .reshape(rows_here, head_count * HEAD_DIM)
        .astype(jnp.bfloat16)
    )
    projected = jnp.dot(context, w_out, preferred_element_type=jnp.float32)
    attended = (hidden_in.astype(jnp.float32) + residual_scale * projected).astype(jnp.bfloat16)
    moe_in = rms_scale(attended, moe_gain)
    moe_in, high_1, high_2 = lax.optimization_barrier((moe_in, high_1, high_2))
    low_3 = swap(low_2, 1)
    high_3 = swap(high_1, 2)
    block_experts = w_gate_up.shape[1]
    group = lax.axis_index("exp") // PIECES
    named = expert_ids[:, :, None] == jnp.arange(ROUTE_LANES, dtype=jnp.int32)[None, None, :]
    routing = jnp.sum(
        jnp.where(named, expert_weights.astype(jnp.float32)[:, :, None], 0.0), axis=1
    ).astype(jnp.bfloat16)
    part = width // REQ_PARTS
    own = lax.axis_index("req")
    sent = [
        lax.dynamic_slice_in_dim(moe_in, (own ^ flip) * part, part, 1)
        for flip in range(REQ_PARTS)
    ]
    gathered = lax.all_gather(
        jnp.concatenate(sent + [routing], axis=1), "exp", axis=0, tiled=True
    )
    first = group * block_experts
    act_low = expert_acts(first, gathered, (low, low_1, low_2, low_3), width)
    act_high = expert_acts(first + half, gathered, (high, high_1, high_2, high_3), width)
    down, low_3, high_3 = lax.optimization_barrier((w_down[0], low_3, high_3))
    down_1, down_2 = swap(down, 1), swap(down, 2)
    act = jnp.concatenate([act_low, act_high], axis=1)
    act, act_low, act_high, down_1, down_2 = lax.optimization_barrier(
        (act, act_low, act_high, down_1, down_2)
    )
    down_3_low = swap(down_2[:half], 1)
    down_3_high = swap(down_1[half:], 2)
    made = [
        jnp.dot(act, flat(rows), preferred_element_type=jnp.float32).astype(jnp.bfloat16)
        for rows in (down, down_1, down_2)
    ]
    made_3 = jnp.dot(act_low, flat(down_3_low), preferred_element_type=jnp.float32) + jnp.dot(
        act_high, flat(down_3_high), preferred_element_type=jnp.float32
    )
    mixed = lax.psum_scatter(
        jnp.concatenate(made + [made_3.astype(jnp.bfloat16)], axis=1),
        "exp",
        scatter_dimension=0,
        tiled=True,
    )
    mixture = jnp.concatenate(
        [
            lax.dynamic_slice_in_dim(mixed, (own ^ flip) * part, part, 1)
            for flip in range(REQ_PARTS)
        ],
        axis=1,
    )
    layer_out = (
        attended.astype(jnp.float32) + residual_scale * mixture.astype(jnp.float32)
    ).astype(jnp.bfloat16)
    return (attended, layer_out)


def swap(values, flip):
    return lax.ppermute(values, "req", [(r, r ^ flip) for r in range(REQ_PARTS)])


def flat(rows):
    return rows.reshape(rows.shape[0] * rows.shape[1], rows.shape[2])


def act_kernel(per_step, first_ref, rows_ref, route_ref, *refs):
    step = pl.program_id(1)
    gate_up_refs, out_ref = refs[:-1], refs[-1]
    slice_width = gate_up_refs[0].shape[2] // 2
    rows = rows_ref[...]
    route = route_ref[...]
    lane = lax.broadcasted_iota(jnp.int32, (ROUTE_LANES, slice_width), 0)
    for k in range(per_step):
        weights = jnp.concatenate([ref[k] for ref in gate_up_refs], axis=0)
        hidden = jnp.dot(rows, weights, preferred_element_type=jnp.float32)
        gate, up = hidden[:, :slice_width], hidden[:, slice_width:]
        pick = (lane == first_ref[0] + step * per_step + k).astype(jnp.bfloat16)
        weight = jnp.dot(route, pick, preferred_element_type=jnp.float32)
        where = slice(k * slice_width, (k + 1) * slice_width)
        out_ref[:, where] = (gate / (1.0 + jnp.exp(-gate)) * up * weight).astype(out_ref.dtype)


def expert_acts(first, gathered, weights, width):
    count = gathered.shape[0]
    tile = min(1024, count)
    experts, depth, wide = weights[0].shape
    slice_width = wide // 2
    per_step = 2 if experts % 2 == 0 else 1
    in_specs = [
        pl.BlockSpec((tile, width), lambda i, s, first: (i, 0)),
        pl.BlockSpec((tile, ROUTE_LANES), lambda i, s, first: (i, width // ROUTE_LANES)),
    ]
    for _ in weights:
        in_specs.append(pl.BlockSpec((per_step, depth, wide), lambda i, s, first: (s, 0, 0)))
    return pl.pallas_call(
        functools.partial(act_kernel, per_step),
        grid_spec=pltpu.PrefetchScalarGridSpec(
            num_scalar_prefetch=1,
            grid=(count // tile, experts // per_step),
            in_specs=in_specs,
            out_specs=pl.BlockSpec((tile, per_step * slice_width), lambda i, s, first: (i, s)),
        ),
        out_shape=jax.ShapeDtypeStruct((count, experts * slice_width), jnp.bfloat16),
        compiler_params=pltpu.CompilerParams(vmem_limit_bytes=40 * 1024 * 1024),
        cost_estimate=pl.CostEstimate(
            flops=2 * count * width * experts * wide,
            bytes_accessed=2 * (experts * width * wide + count * (width + experts * slice_width)),
            transcendentals=count * experts * slice_width,
        ),
    )(jnp.full((1,), first, jnp.int32), gathered, gathered, *weights)


def solution(mesh):
    in_specs = (
        P(("req", "exp"), None),
        P(),
        P(),
        P(),
        P(),
        P(),
        P("req", "exp", None),
        P("req"),
        P(),
        P(("req", "exp"), None),
        P(("req", "exp"), None),
        P("exp", None, "req", None),
        P("exp", None, None, "req"),
    )
    out_specs = (P(("req", "exp"), None), P(("req", "exp"), None))
    return jax.shard_map(shards, mesh=mesh, in_specs=in_specs, out_specs=out_specs, check_vma=False)
```
